512 devices in a mesh: dp: 16 (over x, y), tensor: 32 (over z, core).
Axes of the slice: x: 4, y: 4, z: 16, core: 2. Of those that a mesh axis runs over, the one named last changes fastest.
Arguments:
- query_rows: bfloat16 [2560, 4096], P('dp', 'tensor'), may hold values from -12 to 12
- key_rows: bfloat16 [2560, 4096], P('dp', 'tensor'), may hold values from -12 to 12
- value_rows: bfloat16 [2560, 4096], P('dp', 'tensor'), may hold values from -6 to 6
- out_weight: bfloat16 [4096, 5120], P('tensor'), may hold values from -0.09375 to 0.09375
- encoder: bfloat16 [40, 128, 32], replicated, may hold values from -0.5 to 0.5
- decoder: bfloat16 [40, 32, 128], replicated, may hold values from -1 to 1
- positions: int32 [2560], P('dp'), may hold values from 0 to 159, as said below
- cotangent: bfloat16 [2560, 5120], P(('dp', 'tensor')), may hold values from -1.796875 to 1.796875
Outputs:
- attended: bfloat16 [2560, 5120], P(('dp', 'tensor'))
- grad_query: bfloat16 [2560, 4096], P('dp', 'tensor')
- grad_key: bfloat16 [2560, 4096], P('dp', 'tensor')
- grad_value: bfloat16 [2560, 4096], P('dp', 'tensor')
- grad_weight: bfloat16 [4096, 5120], P('tensor')
The draws below stay inside these ranges and needn't reach their ends.
Inputs may be any that keep to these rules, and one draw needn't show every extreme that they name: `positions`: within each sequence of 160 tokens, the first token has position 0 and every other token's position is 0 or its predecessor's plus one.
All inputs are finite; a program needn't handle non-finite values.
Results may differ from the reference program's by a relative error of at most 0.03.
Values may be sent and summed in bfloat16 or wider, within the bound.
A program may use at most 64 MiB of HBM per device.

```python
import jax
import jax.numpy as jnp
from jax import lax

D = 5120
HEAD = 128
BLOCK = 128
LEN = 160
SEQS = 1
HEADS = 32
NBLK = 40
CB = 32
TOKENS = 2560
N_DP = 16


def doc_positions(key):
    seq_total = TOKENS // LEN
    subkey = jax.random.fold_in(key, 71)
    marks = jax.random.randint(subkey, (seq_total, LEN), 0, 12) == 0
    seq_ids = jnp.arange(seq_total, dtype=jnp.int32)[:, None]
    marks = marks & (seq_ids != 0)
    place = jnp.arange(LEN, dtype=jnp.int32)[None, :]
    starts = jnp.where(marks | (place == 0), place, 0)
    latest = lax.cummax(starts, axis=1)
    return (place - latest).reshape(TOKENS).astype(jnp.int32)


def draw_positions(key, part):
    return doc_positions(key)


def draw_query_rows(key, part):
    key = jax.random.fold_in(key, 3)
    result = jnp.clip(jax.random.normal(key, (TOKENS, HEADS * HEAD)), -12.0, 12.0)
    return result.astype(jnp.bfloat16)


def draw_key_rows(key, part):
    key = jax.random.fold_in(key, 4)
    result = jnp.clip(jax.random.normal(key, (TOKENS, HEADS * HEAD)), -12.0, 12.0)
    return result.astype(jnp.bfloat16)


def block_levels(rng, shape, split, least, high):
    def one(dim, shards_of):
        steps = jax.random.uniform(jax.random.fold_in(jax.random.fold_in(rng, 6), dim), (shards_of,), jnp.float32, least / len(split), high / len(split))
        return jnp.repeat(jnp.exp(steps), shape[dim] // shards_of).reshape((-1,) + (1,) * (len(shape) - dim - 1))

    factor_of = one(*split[0])
    for cut in split[1:]:
        factor_of = factor_of * one(*cut)
    return factor_of


def bell_draw(stream_key, extent, scale, reach, pieces=(), kind=jnp.bfloat16):
    array = jax.random.normal(stream_key, extent, jnp.float32) * scale
    if len(pieces) > 0:
        array = block_levels(stream_key, extent, pieces, -0.22, 0.18) * array
    return jnp.clip(array, min=-reach, max=reach).astype(kind)


def setup_inputs(seed: int = 0) -> dict:
    key_of = jax.random.split(jax.random.key(seed), 9)
    return {
        "query_rows": draw_query_rows(jax.random.fold_in(key_of[8], 71), 0),
        "key_rows": draw_key_rows(jax.random.fold_in(key_of[8], 71), 0),
        "value_rows": bell_draw(key_of[2], (TOKENS, HEADS * HEAD), 1.0, 6.0, ((0, 16), (1, 32))),
        "out_weight": bell_draw(key_of[3], (HEADS * HEAD, D), (HEADS * HEAD) ** -0.5, 0.09375, ((0, 32),)),
        "encoder": bell_draw(key_of[4], (NBLK, BLOCK, CB), BLOCK ** -0.5, 0.5),
        "decoder": bell_draw(key_of[5], (NBLK, CB, BLOCK), CB ** -0.5, 1.0),
        "positions": draw_positions(jax.random.fold_in(key_of[8], 71), 0),
        "cotangent": bell_draw(key_of[7], (TOKENS, D), 0.3, 1.796875, ((0, 512),)),
    }


def encode(partial_value, encoder):
    row_count = partial_value.shape[0]
    blocks, width, narrow = encoder.shape
    shaped = partial_value.reshape(row_count, blocks, width)
    result = jnp.einsum('rbi,bio->rbo', shaped, encoder.astype(jnp.float32), precision=lax.Precision.HIGHEST)
    return result.reshape(row_count, blocks * narrow)


def decode(code_rows, decoder):
    row_count = code_rows.shape[0]
    blocks, narrow, width = decoder.shape
    shaped = code_rows.reshape(row_count, blocks, narrow)
    result = jnp.einsum('rbo,boi->rbi', shaped, decoder.astype(jnp.float32), precision=lax.Precision.HIGHEST)
    return result.reshape(row_count, blocks * width)


def compress(grad_rows, decoder):
    row_count = grad_rows.shape[0]
    blocks, narrow, width = decoder.shape
    shaped = grad_rows.reshape(row_count, blocks, width)
    result = jnp.einsum('rbi,boi->rbo', shaped, decoder.astype(jnp.float32), precision=lax.Precision.HIGHEST)
    return result.reshape(row_count, blocks * narrow)


def expand(code_rows, encoder):
    row_count = code_rows.shape[0]
    blocks, width, narrow = encoder.shape
    shaped = code_rows.reshape(row_count, blocks, narrow)
    result = jnp.einsum('rbo,bio->rbi', shaped, encoder.astype(jnp.float32), precision=lax.Precision.HIGHEST)
    return result.reshape(row_count, blocks * width)


def attend(queries, key_vals, values, doc_pos):
    seq_len = queries.shape[1]
    score_scale = queries.shape[3] ** -0.5
    scores = jnp.einsum('sqhd,skhd->shqk', queries.astype(jnp.float32), key_vals.astype(jnp.float32)) * score_scale
    place = jnp.arange(seq_len, dtype=jnp.int32)
    visible = (place[None, None, :] <= place[None, :, None]) & (place[None, None, :] >= place[None, :, None] - doc_pos[:, :, None])
    scores = jnp.where(visible[:, None], scores, jnp.float32(-1e30))
    largest = jnp.max(scores, axis=-1, keepdims=True)
    exps = jnp.exp(scores - largest)
    attn_prob = exps / jnp.sum(exps, axis=-1, keepdims=True)
    attn_bf = attn_prob.astype(jnp.bfloat16)
    context = jnp.einsum('shqk,skhd->sqhd', attn_bf.astype(jnp.float32), values.astype(jnp.float32)).astype(jnp.bfloat16)
    return attn_prob, attn_bf, context


def attend_back(queries, key_vals, values, attn_prob, attn_bf, grad_context):
    score_scale = queries.shape[3] ** -0.5
    grad_ctx32 = grad_context.astype(jnp.float32)
    grad_value = jnp.einsum('shqk,sqhd->skhd', attn_bf.astype(jnp.float32), grad_ctx32).astype(jnp.bfloat16)
    grad_prob = jnp.einsum('sqhd,skhd->shqk', grad_ctx32, values.astype(jnp.float32))
    row_dot = jnp.sum(attn_prob * grad_prob, axis=-1, keepdims=True)
    grad_score = (attn_prob * (grad_prob - row_dot) * score_scale).astype(jnp.bfloat16).astype(jnp.float32)
    grad_query = jnp.einsum('shqk,skhd->sqhd', grad_score, key_vals.astype(jnp.float32)).astype(jnp.bfloat16)
    grad_key = jnp.einsum('shqk,sqhd->skhd', grad_score, queries.astype(jnp.float32)).astype(jnp.bfloat16)
    return grad_query, grad_key, grad_value


def reference(query_rows, key_rows, value_rows, out_weight, encoder, decoder, positions, cotangent):
    group_rows = SEQS * LEN
    width = HEADS * HEAD

    def one_group(weight_sum, group_idx):
        row_start = (group_idx * group_rows).astype(jnp.int32)
        shape4 = (SEQS, LEN, HEADS, HEAD)
        queries = lax.dynamic_slice_in_dim(query_rows, row_start, group_rows, 0).reshape(shape4)
        key_vals = lax.dynamic_slice_in_dim(key_rows, row_start, group_rows, 0).reshape(shape4)
        values = lax.dynamic_slice_in_dim(value_rows, row_start, group_rows, 0).reshape(shape4)
        doc_pos = lax.dynamic_slice_in_dim(positions, row_start, group_rows, 0).reshape(SEQS, LEN)
        grad_out = lax.dynamic_slice_in_dim(cotangent, row_start, group_rows, 0)
        attn_prob, attn_bf, context4 = attend(queries, key_vals, values, doc_pos)
        context = context4.reshape(group_rows, width)
        partial_value = jnp.dot(context, out_weight, preferred_element_type=jnp.float32)
        attended = decode(encode(partial_value, encoder), decoder).astype(jnp.bfloat16)
        grad_code = compress(grad_out.astype(jnp.float32), decoder).astype(jnp.bfloat16)
        grad_partial = expand(grad_code.astype(jnp.float32), encoder)
        weight_sum = weight_sum + jnp.dot(context.astype(jnp.float32).T, grad_partial, precision=lax.Precision.HIGHEST)
        grad_context = jnp.dot(grad_partial.astype(jnp.bfloat16), out_weight.T, preferred_element_type=jnp.float32).astype(jnp.bfloat16)
        grad_query, grad_key, grad_value = attend_back(queries, key_vals, values, attn_prob, attn_bf, grad_context.reshape(shape4))
        outs_here = (attended, grad_query.reshape(group_rows, width), grad_key.reshape(group_rows, width), grad_value.reshape(group_rows, width))
        return weight_sum, outs_here

    start_sum = jnp.zeros((width, D), jnp.float32)
    weight_sum, stacked = lax.scan(one_group, start_sum, jnp.arange(N_DP, dtype=jnp.int32))
    attended = stacked[0].reshape(TOKENS, D)
    grad_query = stacked[1].reshape(TOKENS, width)
    grad_key = stacked[2].reshape(TOKENS, width)
    grad_value = stacked[3].reshape(TOKENS, width)
    return attended, grad_query, grad_key, grad_value, weight_sum.astype(jnp.bfloat16)
```

```python
import functools

import jax
import jax.numpy as jnp
from jax import lax
from jax.experimental import pallas as pl
from jax.experimental.pallas import tpu as pltpu
from jax.sharding import PartitionSpec as P

MESH = pl.DeviceIdType.MESH
F32 = jnp.float32
BF16 = jnp.bfloat16

LEN = 160
HEAD = 128
WIDTH = 5120
CODE = 1280
TILES = CODE // 128
OWN = 5
PAD = 8
SLOTS = 32
MSG = 64
DP = 16
NT = (((1,), (1,)), ((), ()))
TN = (((0,), (0,)), ((), ()))


def dot(a, b, dims=(((1,), (0,)), ((), ()))):
    return lax.dot_general(a, b, dims, preferred_element_type=F32)


def lane_groups(rows):
    return lax.broadcasted_iota(jnp.int32, (rows, 128), 1) // 32


def core_kernel(
    q_hbm, k_hbm, v_hbm, w_hbm, enc_hbm, dec_hbm, pos_hbm, cot_hbm,
    sum_out, att_out, gq_out, gk_out, gv_out, enc,
    q, k, v, w, dec, pos, cot, cot8, gst, gbuf, ust, gpad, perm, attn, ctx, ctx_t, spread, wenc,
    pst, psnd, psib, pone, prec1, ptwo, prec2, code, mpart, mrecv, mfull,
    in_sem, send_sem, recv_sem,
):
    dp = lax.axis_index("dp")
    t = lax.axis_index("tensor")
    core = lax.rem(t, 2)
    sign = 1 - 2 * core

    def chip(dz):
        return {"tensor": lax.rem(t + 2 * dz + SLOTS, SLOTS)}

    sibling = {"tensor": t + sign}

    def plane(d):
        return {"dp": lax.rem(dp + d, DP)}

    loads = []
    for n, (src, dst) in enumerate(
        ((cot_hbm, cot), (dec_hbm, dec), (q_hbm, q), (k_hbm, k), (v_hbm, v), (pos_hbm, pos), (enc_hbm, enc), (w_hbm, w))
    ):
        c = pltpu.make_async_copy(src, dst, in_sem.at[n])
        c.start()
        loads.append(c)
    cot_in, dec_in, q_in, k_in, v_in, pos_in, enc_in, w_in = loads

    barrier = pltpu.get_barrier_semaphore()
    partners = [sibling] + [chip(dz) for dz in (8, 4, -4, 2, -2, 1, -1)] + [plane(d) for d in range(1, DP)]
    for device in partners:
        pl.semaphore_signal(barrier, inc=1, device_id=device, device_id_type=MESH)

    count = [0]
    started = []

    def send(src, dst, device):
        n = count[0]
        count[0] = n + 1
        c = pltpu.make_async_remote_copy(
            src_ref=src, dst_ref=dst, send_sem=send_sem.at[n], recv_sem=recv_sem.at[n],
            device_id=device, device_id_type=MESH,
        )
        c.start()
        started.append(c)
        return c

    cot8[...] = jnp.zeros_like(cot8)
    gst[...] = jnp.zeros_like(gst)
    groups8 = lane_groups(PAD)
    cot_in.wait()
    dec_in.wait()
    cot8[0:OWN, :] = cot[...].astype(F32)
    for j in range(TILES):
        rows = jnp.concatenate([cot8[:, 512 * j + 128 * i : 512 * j + 128 * (i + 1)] for i in range(4)], axis=0)
        full = dot(rows.astype(BF16), dec[4 * j : 4 * j + 4].reshape(128, 128), NT)
        tile = jnp.zeros((PAD, 128), F32)
        for i in range(4):
            tile = tile + jnp.where(groups8 == i, full[PAD * i : PAD * (i + 1)], 0.0)
        gst[OWN * j : OWN * j + PAD, :] = tile
    gbuf[0, 0, 0] = gst[...].astype(BF16)

    pl.semaphore_wait(barrier, len(partners))

    steps = (0, 1, 2 * sign, -1)
    g_far = [None] + [send(gbuf.at[0, 0, 0], gbuf.at[0, 0, 4 - n], chip(4 * n)) for n in (2, 1, 3)]
    g_near = [None] + [send(gbuf.at[0, 0, 0], gbuf.at[0, p, 0], chip(-steps[p])) for p in (1, 2, 3)]

    row = lax.broadcasted_iota(jnp.int32, (SLOTS * PAD, LEN), 0)
    col = lax.broadcasted_iota(jnp.int32, (SLOTS * PAD, LEN), 1)
    slot = row // PAD
    other = slot // 16
    near = (slot // 4) % 4
    far = slot % 4
    step = jnp.where(near == 1, 1, jnp.where(near == 2, 2 * sign * (1 - 2 * other), jnp.where(near == 3, -1, 0)))
    at_chip = (t // 2 + step + 4 * far + 16) % 16
    token = OWN * (2 * at_chip + (core + other) % 2) + row % PAD
    valid = row % PAD < OWN
    perm[...] = jnp.where(valid & (token == col), 1.0, 0.0).astype(BF16)

    q_in.wait()
    k_in.wait()
    v_in.wait()
    pos_in.wait()
    scale = HEAD ** (-0.5)
    qp = dot(perm[...], q[...]).astype(BF16)
    pos8 = jnp.broadcast_to(pos[...].reshape(1, LEN), (PAD, LEN)).astype(F32).astype(BF16)
    pos_col = dot(perm[...], pos8, NT)[:, 0:1].astype(jnp.int32)
    scores = dot(qp, k[...], NT) * scale
    visible = (col <= token) & (col >= token - pos_col)
    scores = jnp.where(visible, scores, F32(-1e30))
    exps = jnp.exp(scores - jnp.max(scores, axis=-1, keepdims=True))
    probs = exps / jnp.sum(exps, axis=-1, keepdims=True)
    attn[...] = probs
    ctx_f = dot(probs.astype(BF16), v[...])
    ctx[...] = ctx_f.astype(BF16)
    ctx_t[...] = ctx_f.T.astype(BF16)

    enc_in.wait()
    code_group = lax.broadcasted_iota(jnp.int32, (128, 128), 0) // 32
    for j in range(TILES):
        group = enc[4 * j : 4 * j + 4].reshape(128, 128)
        for i in range(4):
            spread[j, :, 128 * i : 128 * (i + 1)] = jnp.where(code_group == i, group, jnp.zeros_like(group))

    w_in.wait()
    for j in range(TILES):
        part = dot(w[:, 512 * j : 512 * (j + 1)], spread[j], NT).astype(BF16)
        wenc[:, 128 * j : 128 * (j + 1)] = part
        pst[:, OWN * j : OWN * j + PAD, :] = dot(ctx[...], part).reshape(SLOTS, PAD, 128)
    pst[:, MSG - 8 : MSG, :] = jnp.zeros((SLOTS, 8, 128), F32)
    psnd[...] = pst[16:32].reshape(4, 4, MSG, 128).astype(BF16)
    p_sib = send(psnd, psib, sibling)

    for c in g_far[1:]:
        c.wait_recv()
    g_pack = [None] + [send(gbuf.at[0, 0, pl.ds(1, 3)], gbuf.at[0, p, pl.ds(1, 3)], chip(-steps[p])) for p in (1, 2, 3)]
    g_over = [send(gbuf.at[0, 0], gbuf.at[1, 0], sibling)]

    p_sib.wait_recv()
    for p in range(4):
        pst[4 * p : 4 * p + 4] = pst[4 * p : 4 * p + 4] + psib[p].astype(F32)
        if p:
            pone[p] = pst[4 * p : 4 * p + 4].astype(BF16)
    p_near = [None] + [send(pone.at[p], prec1.at[p], chip(steps[p])) for p in (1, 2, 3)]

    def unpack(other_core):
        for p in range(4):
            ust[4 * p : 4 * p + 4] = gbuf[other_core, p].astype(F32)
        keep = lax.broadcasted_iota(jnp.int32, (16, PAD, 128), 1) < OWN
        for j in range(TILES):
            block = jnp.where(keep, ust[:, OWN * j : OWN * j + PAD, :], 0.0)
            gpad[128 * other_core : 128 * (other_core + 1), 128 * j : 128 * (j + 1)] = block.reshape(128, 128).astype(BF16)

    for p in (1, 3, 2):
        g_near[p].wait_recv()
        g_pack[p].wait_recv()
        g_over.append(send(gbuf.at[0, p], gbuf.at[1, p], sibling))
    unpack(0)
    for c in g_over:
        c.wait_recv()
    unpack(1)

    for half in range(2):
        part = dot(ctx_t[...], gpad[:, 640 * half : 640 * (half + 1)]).astype(BF16)
        for r in range(8):
            mpart[2 * r + half] = part[16 * r : 16 * (r + 1)]
    m_parts = []
    for d in range(1, DP):
        m_parts.append(send(mpart.at[lax.rem(dp + d, DP)], mrecv.at[d], plane(d)))

    for c in p_near[1:]:
        c.wait_recv()
    for n in range(4):
        total = pst[n]
        for p in (1, 2, 3):
            total = total + prec1[p, n].astype(F32)
        if n:
            ptwo[n] = total.astype(BF16)
        else:
            code[0:MSG] = total
    p_far = [None] + [send(ptwo.at[n], prec2.at[n], chip(4 * n)) for n in (2, 1, 3)]

    gc = dot(gpad[...], wenc[...], NT).astype(BF16)
    probs = attn[...]
    gv_out[...] = dot(probs.astype(BF16), gc, TN).astype(BF16)
    g_prob = dot(gc, v[...], NT)
    row_dot = jnp.sum(probs * g_prob, axis=-1, keepdims=True)
    g_score = (probs * (g_prob - row_dot) * scale).astype(BF16)
    gq_out[...] = dot(perm[...], dot(g_score, k[...]).astype(BF16), TN).astype(BF16)
    gk_out[...] = dot(g_score, qp, TN).astype(BF16)

    for c in m_parts:
        c.wait_recv()
    total = mpart[dp].astype(F32)
    for d in range(1, DP):
        total = total + mrecv[d].astype(F32)
    mfull[dp] = total.astype(BF16)
    m_sums = [send(mfull.at[dp], mfull.at[dp], plane(d)) for d in range(1, DP)]

    for c in p_far[1:]:
        c.wait_recv()
    total = code[0:MSG]
    for n in (1, 2, 3):
        total = total + prec2[n].astype(F32)
    code[0:MSG] = total
    for j in range(TILES):
        rows = code[OWN * j : OWN * j + PAD, :]
        rows = jnp.concatenate([jnp.where(groups8 == i, rows, 0.0) for i in range(4)], axis=0)
        full = dot(rows.astype(BF16), dec[4 * j : 4 * j + 4].reshape(128, 128))
        for i in range(4):
            att_out[:, 512 * j + 128 * i : 512 * j + 128 * (i + 1)] = full[PAD * i : PAD * i + OWN].astype(BF16)

    for c in m_sums:
        c.wait_recv()
    sum_out[...] = mfull[...]
    for c in started:
        c.wait_send()


def weight_kernel(sums, enc, att_in, gq_in, gk_in, gv_in, att_out, gq_out, gk_out, gv_out, gw_out, gw, out_sem):
    saves = []
    for n, (src, dst) in enumerate(((att_in, att_out), (gq_in, gq_out), (gk_in, gk_out), (gv_in, gv_out))):
        c = pltpu.make_async_copy(src, dst, out_sem.at[n])
        c.start()
        saves.append(c)
    groups = lane_groups(HEAD)
    for j in range(TILES):
        half, place = j // 5, j % 5
        rows = jnp.concatenate([sums[2 * r + half, :, 128 * place : 128 * (place + 1)] for r in range(8)], axis=0)
        block = enc[4 * j : 4 * j + 4].reshape(128, 128)
        for i in range(4):
            gw[j, :, 128 * i : 128 * (i + 1)] = dot(jnp.where(groups == i, rows, jnp.zeros_like(rows)), block).astype(BF16)
        c = pltpu.make_async_copy(gw.at[j], gw_out.at[:, pl.ds(512 * j, 512)], out_sem.at[4 + j])
        c.start()
        saves.append(c)
    for c in saves:
        c.wait()


def local(q, k, v, w, enc, dec, pos, cot):
    any_ = pl.BlockSpec(memory_space=pl.ANY)
    hbm = pl.BlockSpec(memory_space=pltpu.HBM)
    vmem = pl.BlockSpec(memory_space=pltpu.VMEM)

    def shape(*dims):
        return jax.ShapeDtypeStruct(dims, BF16)

    n_copies = 50
    operands = (q, k, v, w, enc.transpose(0, 2, 1), dec, pos, cot)
    row_shapes = (shape(OWN, WIDTH), shape(LEN, HEAD), shape(LEN, HEAD), shape(LEN, HEAD))
    sums, att, gq, gk, gv, enc_kept = pl.pallas_call(
        core_kernel,
        out_shape=(shape(DP, 16, 640), *row_shapes, shape(40, 32, 128)),
        in_specs=[hbm] * 8,
        out_specs=[vmem] * 6,
        scratch_shapes=[
            pltpu.VMEM((LEN, HEAD), BF16),
            pltpu.VMEM((LEN, HEAD), BF16),
            pltpu.VMEM((LEN, HEAD), BF16),
            pltpu.VMEM((HEAD, WIDTH), BF16),
            pltpu.VMEM((40, 32, 128), BF16),
            pltpu.VMEM((LEN,), jnp.int32),
            pltpu.VMEM((OWN, WIDTH), BF16),
            pltpu.VMEM((PAD, WIDTH), F32),
            pltpu.VMEM((MSG, 128), F32),
            pltpu.VMEM((2, 4, 4, MSG, 128), BF16),
            pltpu.VMEM((16, MSG, 128), F32),
            pltpu.VMEM((SLOTS * PAD, CODE), BF16),
            pltpu.VMEM((SLOTS * PAD, LEN), BF16),
            pltpu.VMEM((SLOTS * PAD, LEN), F32),
            pltpu.VMEM((SLOTS * PAD, HEAD), BF16),
            pltpu.VMEM((HEAD, SLOTS * PAD), BF16),
            pltpu.VMEM((TILES, 128, 512), BF16),
            pltpu.VMEM((HEAD, CODE), BF16),
            pltpu.VMEM((SLOTS, MSG, 128), F32),
            pltpu.VMEM((4, 4, MSG, 128), BF16),
            pltpu.VMEM((4, 4, MSG, 128), BF16),
            pltpu.VMEM((4, 4, MSG, 128), BF16),
            pltpu.VMEM((4, 4, MSG, 128), BF16),
            pltpu.VMEM((4, MSG, 128), BF16),
            pltpu.VMEM((4, MSG, 128), BF16),
            pltpu.VMEM((MSG, 128), F32),
            pltpu.VMEM((DP, 16, 640), BF16),
            pltpu.VMEM((DP, 16, 640), BF16),
            pltpu.VMEM((DP, 16, 640), BF16),
            pltpu.SemaphoreType.DMA((8,)),
            pltpu.SemaphoreType.DMA((n_copies,)),
            pltpu.SemaphoreType.DMA((n_copies,)),
        ],
        compiler_params=pltpu.CompilerParams(
            collective_id=0, has_side_effects=True, vmem_limit_bytes=48 * 2**20
        ),
        name="attention_and_sums",
    )(*[pltpu.with_memory_space_constraint(a, pltpu.HBM) for a in operands])
    return pl.pallas_call(
        weight_kernel,
        out_shape=(*row_shapes, shape(HEAD, WIDTH)),
        in_specs=[vmem] * 6,
        out_specs=[any_] * 5,
        scratch_shapes=[
            pltpu.VMEM((TILES, HEAD, 512), BF16),
            pltpu.SemaphoreType.DMA((4 + TILES,)),
        ],
        compiler_params=pltpu.CompilerParams(vmem_limit_bytes=16 * 2**20),
        name="weight_gradient",
    )(sums, enc_kept, att, gq, gk, gv)


def solution(mesh):
    return jax.shard_map(
        local,
        mesh=mesh,
        in_specs=(
            P("dp", "tensor"), P("dp", "tensor"), P("dp", "tensor"), P("tensor", None),
            P(), P(), P("dp"), P(("dp", "tensor"), None),
        ),
        out_specs=(
            P(("dp", "tensor"), None), P("dp", "tensor"), P("dp", "tensor"), P("dp", "tensor"), P("tensor", None),
        ),
        check_vma=False,
    )
```

```python
import functools

import jax
import jax.numpy as jnp
from jax import lax
from jax.experimental import pallas as pl
from jax.experimental.pallas import tpu as pltpu
from jax.sharding import PartitionSpec as P

MESH = pl.DeviceIdType.MESH
F32 = jnp.float32
BF16 = jnp.bfloat16

LEN = 160
HEAD = 128
WIDTH = 5120
CODE = 1280
TILES = CODE // 128
OWN = 5
PAD = 8
SLOTS = 32
MSG = 64
DP = 16
NT = (((1,), (1,)), ((), ()))
TN = (((0,), (0,)), ((), ()))
NEAR = (0, 1, -1)
FAR = (0, 3, -3, 6, -6)


def dot(a, b, dims=(((1,), (0,)), ((), ()))):
    return lax.dot_general(a, b, dims, preferred_element_type=F32)


def lane_groups(rows):
    return lax.broadcasted_iota(jnp.int32, (rows, 128), 1) // 32


def core_kernel(
    q_hbm, k_hbm, v_hbm, w_hbm, enc_hbm, dec_hbm, pos_hbm, cot_hbm,
    sum_a_out, sum_b_out, att_out, gq_out, gk_out, gv_out, enc,
    q, k, v, w, dec, pos, cot, cot8, gst, gbuf, ust, gpad, perm, attn, ctx, ctx_t, spread, wenc,
    pst, psnd, psib, pone, prec1, prec15, ptwo, prec2, code, part_a, part_b, recv_a, recv_b, full_a, full_b,
    in_sem, send_sem, recv_sem,
):
    dp = lax.axis_index("dp")
    t = lax.axis_index("tensor")
    core = lax.rem(t, 2)
    sign = 1 - 2 * core

    def chip(dz):
        return {"tensor": lax.rem(t + 2 * dz + SLOTS, SLOTS)}

    sibling = {"tensor": t + sign}

    def plane_at(d):
        return lax.rem(dp // 4 + d // 4, 4) * 4 + lax.rem(dp + d, 4)

    def plane(d):
        return {"dp": plane_at(d)}

    offsets = sorted(range(1, DP), key=lambda d: -min(d // 4, 4 - d // 4) - min(d % 4, 4 - d % 4))

    loads = []
    for n, (src, dst) in enumerate(
        ((cot_hbm, cot), (dec_hbm, dec), (q_hbm, q), (k_hbm, k), (v_hbm, v), (pos_hbm, pos), (enc_hbm, enc), (w_hbm, w))
    ):
        c = pltpu.make_async_copy(src, dst, in_sem.at[n])
        c.start()
        loads.append(c)
    cot_in, dec_in, q_in, k_in, v_in, pos_in, enc_in, w_in = loads

    barrier = pltpu.get_barrier_semaphore()
    partners = [sibling] + [chip(dz) for dz in (6, -6, 3, -3, 2, -2, 1, -1)] + [plane(d) for d in offsets]
    for device in partners:
        pl.semaphore_signal(barrier, inc=1, device_id=device, device_id_type=MESH)

    count = [0]
    started = []

    def send(src, dst, device):
        n = count[0]
        count[0] = n + 1
        c = pltpu.make_async_remote_copy(
            src_ref=src, dst_ref=dst, send_sem=send_sem.at[n], recv_sem=recv_sem.at[n],
            device_id=device, device_id_type=MESH,
        )
        c.start()
        started.append(c)
        return c

    cot8[...] = jnp.zeros_like(cot8)
    gst[...] = jnp.zeros_like(gst)
    groups8 = lane_groups(PAD)
    cot_in.wait()
    dec_in.wait()
    cot8[0:OWN, :] = cot[...].astype(F32)
    for j in range(TILES):
        rows = jnp.concatenate([cot8[:, 512 * j + 128 * i : 512 * j + 128 * (i + 1)] for i in range(4)], axis=0)
        full = dot(rows.astype(BF16), dec[4 * j : 4 * j + 4].reshape(128, 128), NT)
        tile = jnp.zeros((PAD, 128), F32)
        for i in range(4):
            tile = tile + jnp.where(groups8 == i, full[PAD * i : PAD * (i + 1)], 0.0)
        gst[OWN * j : OWN * j + PAD, :] = tile
    gbuf[0, 0] = gst[...].astype(BF16)

    row = lax.broadcasted_iota(jnp.int32, (SLOTS * PAD, LEN), 0)
    col = lax.broadcasted_iota(jnp.int32, (SLOTS * PAD, LEN), 1)
    slot = row // PAD
    other = slot // 16
    place = slot % 16
    step = jnp.full_like(row, 8)
    for n in range(15):
        step = jnp.where(place == n, NEAR[n // 5] + FAR[n % 5], step)
    at_chip = (t // 2 + step + 16) % 16
    token = OWN * (2 * at_chip + (core + other) % 2) + row % PAD
    valid = row % PAD < OWN
    perm[...] = jnp.where(valid & (token == col), 1.0, 0.0).astype(BF16)

    q_in.wait()
    k_in.wait()
    v_in.wait()
    pos_in.wait()
    scale = HEAD ** (-0.5)
    qp = dot(perm[...], q[...]).astype(BF16)
    pos8 = jnp.broadcast_to(pos[...].reshape(1, LEN), (PAD, LEN)).astype(F32).astype(BF16)
    pos_col = dot(perm[...], pos8, NT)[:, 0:1].astype(jnp.int32)
    scores = dot(qp, k[...], NT) * scale
    visible = (col <= token) & (col >= token - pos_col)
    scores = jnp.where(visible, scores, F32(-1e30))
    exps = jnp.exp(scores - jnp.max(scores, axis=-1, keepdims=True))
    probs = exps / jnp.sum(exps, axis=-1, keepdims=True)
    attn[...] = probs
    ctx_f = dot(probs.astype(BF16), v[...])
    ctx[...] = ctx_f.astype(BF16)
    ctx_t[...] = ctx_f.T.astype(BF16)

    enc_in.wait()
    code_group = lax.broadcasted_iota(jnp.int32, (128, 128), 0) // 32
    for j in range(TILES):
        group = enc[4 * j : 4 * j + 4].reshape(128, 128)
        for i in range(4):
            spread[j, :, 128 * i : 128 * (i + 1)] = jnp.where(code_group == i, group, jnp.zeros_like(group))

    w_in.wait()
    for j in range(TILES):
        part = dot(w[:, 512 * j : 512 * (j + 1)], spread[j], NT).astype(BF16)
        wenc[:, 128 * j : 128 * (j + 1)] = part
    for j in range(TILES):
        part = dot(ctx[...], wenc[:, 128 * j : 128 * (j + 1)])
        pst[:, OWN * j : OWN * j + PAD, :] = part.reshape(SLOTS, PAD, 128)
    pst[:, MSG - 8 : MSG, :] = jnp.zeros((SLOTS, 8, 128), F32)
    psnd[...] = pst[16:32].astype(BF16)
    pl.semaphore_wait(barrier, len(partners))

    own = gbuf.at[0, 0]
    g_far = {}
    for n in (3, 4, 1, 2):
        back = n + 1 if n % 2 else n - 1
        g_far[n] = send(own, gbuf.at[0, back], chip(FAR[n]))
    g_near = {p: send(own, gbuf.at[0, 5 * p], chip(-NEAR[p])) for p in (1, 2)}
    p_sib = send(psnd, psib, sibling)

    p_sib.wait_recv()
    for n in range(16):
        pst[n] = pst[n] + psib[n].astype(F32)
        if n >= 5:
            pone[n] = pst[n].astype(BF16)
    p_near = [send(pone.at[pl.ds(5 * p, 5)], prec1.at[p], chip(NEAR[p])) for p in (1, 2)]
    p_near.append(send(pone.at[15], prec15, chip(2 * sign)))

    def unpack(other_core):
        ust[...] = gbuf[other_core].astype(F32)
        keep = lax.broadcasted_iota(jnp.int32, (16, PAD, 128), 1) < OWN
        for j in range(TILES):
            block = jnp.where(keep, ust[:, OWN * j : OWN * j + PAD, :], 0.0)
            gpad[128 * other_core : 128 * (other_core + 1), 128 * j : 128 * (j + 1)] = block.reshape(128, 128).astype(BF16)

    g_pack = {}
    for part in (1, 3):
        g_far[part].wait_recv()
        g_far[part + 1].wait_recv()
        for p in (1, 2):
            block = pl.ds(5 * p + part, 2)
            g_pack[p, part] = send(gbuf.at[0, pl.ds(part, 2)], gbuf.at[0, block], chip(-NEAR[p]))
    g_last = send(gbuf.at[0, 3 + core], gbuf.at[0, 15], chip(-2 * sign))
    g_over = [send(gbuf.at[0, pl.ds(0, 5)], gbuf.at[1, pl.ds(0, 5)], sibling)]
    for c in p_near:
        c.wait_recv()
    for n in range(5):
        total = pst[n] + prec1[1, n].astype(F32) + prec1[2, n].astype(F32)
        if n >= 3:
            total = total + jnp.where(core == n - 3, prec15[...].astype(F32), 0.0)
        if n:
            ptwo[n] = total.astype(BF16)
        else:
            code[0:MSG] = total
    p_far = [send(ptwo.at[n], prec2.at[n], chip(FAR[n])) for n in (3, 4, 1, 2)]
    for p in (1, 2):
        g_near[p].wait_recv()
        g_pack[p, 1].wait_recv()
        g_over.append(send(gbuf.at[0, pl.ds(5 * p, 3)], gbuf.at[1, pl.ds(5 * p, 3)], sibling))
    for p in (1, 2):
        g_pack[p, 3].wait_recv()
        g_over.append(send(gbuf.at[0, pl.ds(5 * p + 3, 2)], gbuf.at[1, pl.ds(5 * p + 3, 2)], sibling))
    g_last.wait_recv()
    g_over.append(send(gbuf.at[0, 15], gbuf.at[1, 15], sibling))
    unpack(0)
    for c in g_over:
        c.wait_recv()
    unpack(1)

    m_parts = []
    for start, width, part, recv in ((0, 768, part_a, recv_a), (768, 512, part_b, recv_b)):
        grad = dot(ctx_t[...], gpad[:, start : start + width]).astype(BF16)
        for r in range(DP):
            part[r] = grad[16 * (r // 2) : 16 * (r // 2 + 1), width // 2 * (r % 2) : width // 2 * (r % 2 + 1)]
        m_parts.append([send(part.at[plane_at(d)], recv.at[d], plane(d)) for d in offsets])

    gc = dot(gpad[...], wenc[...], NT).astype(BF16)
    probs = attn[...]
    gv_out[...] = dot(probs.astype(BF16), gc, TN).astype(BF16)
    g_prob = dot(gc, v[...], NT)
    row_dot = jnp.sum(probs * g_prob, axis=-1, keepdims=True)
    g_score = (probs * (g_prob - row_dot) * scale).astype(BF16)
    gq_out[...] = dot(perm[...], dot(g_score, k[...]).astype(BF16), TN).astype(BF16)
    gk_out[...] = dot(g_score, qp, TN).astype(BF16)

    m_sums = []
    for copies, part, recv, full in ((m_parts[0], part_a, recv_a, full_a), (m_parts[1], part_b, recv_b, full_b)):
        total = part[dp].astype(F32)
        for d, c in zip(offsets, copies):
            c.wait_recv()
            total = total + recv[d].astype(F32)
        full[dp] = total.astype(BF16)
        m_sums += [send(full.at[dp], full.at[dp], plane(d)) for d in offsets]

    for c in p_far:
        c.wait_recv()
    total = code[0:MSG]
    for n in (1, 2, 3, 4):
        total = total + prec2[n].astype(F32)
    code[0:MSG] = total
    for j in range(TILES):
        rows = code[OWN * j : OWN * j + PAD, :]
        rows = jnp.concatenate([jnp.where(groups8 == i, rows, 0.0) for i in range(4)], axis=0)
        full = dot(rows.astype(BF16), dec[4 * j : 4 * j + 4].reshape(128, 128))
        for i in range(4):
            att_out[:, 512 * j + 128 * i : 512 * j + 128 * (i + 1)] = full[PAD * i : PAD * i + OWN].astype(BF16)

    for c in m_sums:
        c.wait_recv()
    sum_a_out[...] = full_a[...]
    sum_b_out[...] = full_b[...]
    for c in started:
        c.wait_send()


def weight_kernel(sum_a, sum_b, enc, att_in, gq_in, gk_in, gv_in, att_out, gq_out, gk_out, gv_out, gw_out, gw, out_sem):
    saves = []
    for n, (src, dst) in enumerate(((att_in, att_out), (gq_in, gq_out), (gk_in, gk_out), (gv_in, gv_out))):
        c = pltpu.make_async_copy(src, dst, out_sem.at[n])
        c.start()
        saves.append(c)
    groups = lane_groups(HEAD)
    for j in range(TILES):
        sums, wide, at = (sum_a, 3, j) if j < 6 else (sum_b, 2, j - 6)
        half, place = at // wide, at % wide
        rows = jnp.concatenate([sums[2 * r + half, :, 128 * place : 128 * (place + 1)] for r in range(8)], axis=0)
        block = enc[4 * j : 4 * j + 4].reshape(128, 128)
        for i in range(4):
            gw[j, :, 128 * i : 128 * (i + 1)] = dot(jnp.where(groups == i, rows, jnp.zeros_like(rows)), block).astype(BF16)
        c = pltpu.make_async_copy(gw.at[j], gw_out.at[:, pl.ds(512 * j, 512)], out_sem.at[4 + j])
        c.start()
        saves.append(c)
    for c in saves:
        c.wait()


def local(q, k, v, w, enc, dec, pos, cot):
    any_ = pl.BlockSpec(memory_space=pl.ANY)
    hbm = pl.BlockSpec(memory_space=pltpu.HBM)
    vmem = pl.BlockSpec(memory_space=pltpu.VMEM)

    def shape(*dims):
        return jax.ShapeDtypeStruct(dims, BF16)

    n_copies = 85
    operands = (q, k, v, w, enc.transpose(0, 2, 1), dec, pos, cot)
    row_shapes = (shape(OWN, WIDTH), shape(LEN, HEAD), shape(LEN, HEAD), shape(LEN, HEAD))
    sum_a, sum_b, att, gq, gk, gv, enc_kept = pl.pallas_call(
        core_kernel,
        out_shape=(shape(DP, 16, 384), shape(DP, 16, 256), *row_shapes, shape(40, 32, 128)),
        in_specs=[hbm] * 8,
        out_specs=[vmem] * 7,
        scratch_shapes=[
            pltpu.VMEM((LEN, HEAD), BF16),
            pltpu.VMEM((LEN, HEAD), BF16),
            pltpu.VMEM((LEN, HEAD), BF16),
            pltpu.VMEM((HEAD, WIDTH), BF16),
            pltpu.VMEM((40, 32, 128), BF16),
            pltpu.VMEM((LEN,), jnp.int32),
            pltpu.VMEM((OWN, WIDTH), BF16),
            pltpu.VMEM((PAD, WIDTH), F32),
            pltpu.VMEM((MSG, 128), F32),
            pltpu.VMEM((2, 16, MSG, 128), BF16),
            pltpu.VMEM((16, MSG, 128), F32),
            pltpu.VMEM((SLOTS * PAD, CODE), BF16),
            pltpu.VMEM((SLOTS * PAD, LEN), BF16),
            pltpu.VMEM((SLOTS * PAD, LEN), F32),
            pltpu.VMEM((SLOTS * PAD, HEAD), BF16),
            pltpu.VMEM((HEAD, SLOTS * PAD), BF16),
            pltpu.VMEM((TILES, 128, 512), BF16),
            pltpu.VMEM((HEAD, CODE), BF16),
            pltpu.VMEM((SLOTS, MSG, 128), F32),
            pltpu.VMEM((16, MSG, 128), BF16),
            pltpu.VMEM((16, MSG, 128), BF16),
            pltpu.VMEM((16, MSG, 128), BF16),
            pltpu.VMEM((3, 5, MSG, 128), BF16),
            pltpu.VMEM((MSG, 128), BF16),
            pltpu.VMEM((5, MSG, 128), BF16),
            pltpu.VMEM((5, MSG, 128), BF16),
            pltpu.VMEM((MSG, 128), F32),
            pltpu.VMEM((DP, 16, 384), BF16),
            pltpu.VMEM((DP, 16, 256), BF16),
            pltpu.VMEM((DP, 16, 384), BF16),
            pltpu.VMEM((DP, 16, 256), BF16),
            pltpu.VMEM((DP, 16, 384), BF16),
            pltpu.VMEM((DP, 16, 256), BF16),
            pltpu.SemaphoreType.DMA((8,)),
            pltpu.SemaphoreType.DMA((n_copies,)),
            pltpu.SemaphoreType.DMA((n_copies,)),
        ],
        compiler_params=pltpu.CompilerParams(
            collective_id=0, has_side_effects=True, vmem_limit_bytes=48 * 2**20
        ),
        name="attention_and_sums",
    )(*[pltpu.with_memory_space_constraint(a, pltpu.HBM) for a in operands])
    return pl.pallas_call(
        weight_kernel,
        out_shape=(*row_shapes, shape(HEAD, WIDTH)),
        in_specs=[vmem] * 7,
        out_specs=[any_] * 5,
        scratch_shapes=[
            pltpu.VMEM((TILES, HEAD, 512), BF16),
            pltpu.SemaphoreType.DMA((4 + TILES,)),
        ],
        compiler_params=pltpu.CompilerParams(vmem_limit_bytes=16 * 2**20),
        name="weight_gradient",
    )(sum_a, sum_b, enc_kept, att, gq, gk, gv)


def solution(mesh):
    return jax.shard_map(
        local,
        mesh=mesh,
        in_specs=(
            P("dp", "tensor"), P("dp", "tensor"), P("dp", "tensor"), P("tensor", None),
            P(), P(), P("dp"), P(("dp", "tensor"), None),
        ),
        out_specs=(
            P(("dp", "tensor"), None), P("dp", "tensor"), P("dp", "tensor"), P("dp", "tensor"), P("tensor", None),
        ),
        check_vma=False,
    )
```

```python
import functools

import jax
import jax.numpy as jnp
from jax import lax
from jax.experimental import pallas as pl
from jax.experimental.pallas import tpu as pltpu
from jax.sharding import PartitionSpec as P

MESH = pl.DeviceIdType.MESH
F32 = jnp.float32
BF16 = jnp.bfloat16

LEN = 160
HEAD = 128
WIDTH = 5120
CODE = 1280
TILES = CODE // 128
OWN = 5
PAD = 8
SLOTS = 32
MSG = 64
DP = 16
NT = (((1,), (1,)), ((), ()))
TN = (((0,), (0,)), ((), ()))
NEAR = (0, 1, -1)
FAR = (0, 3, -3, 6, -6)
PARTS = ((0, 4), (4, 6))
LAST = len(PARTS) - 1


def dot(a, b, dims=(((1,), (0,)), ((), ()))):
    return lax.dot_general(a, b, dims, preferred_element_type=F32)


def lane_groups(rows):
    return lax.broadcasted_iota(jnp.int32, (rows, 128), 1) // 32


def expand(sums, wide, at, block):
    half, place = at // wide, at % wide
    rows = jnp.concatenate([sums[2 * r + half, :, 128 * place : 128 * (place + 1)] for r in range(8)], axis=0)
    groups = lane_groups(HEAD)
    return [dot(jnp.where(groups == i, rows, jnp.zeros_like(rows)), block).astype(BF16) for i in range(4)]


def core_kernel(
    q_hbm, k_hbm, v_hbm, w_hbm, enc_hbm, dec_hbm, pos_hbm, cot_hbm,
    gw_out, last_out, att_out, gq_out, gk_out, gv_out, enc,
    q, k, v, w, dec, pos, cot, cot8, gst, gbuf, ust, gpad, perm, attn, ctx, ctx_t, spread, wenc,
    pst, psnd, psib, pone, prec1, prec15, ptwo, prec2, code, *rest,
):
    n_parts = len(PARTS)
    parts, recvs, fulls = rest[:n_parts], rest[n_parts : 2 * n_parts], rest[2 * n_parts : 3 * n_parts]
    in_sem, send_sem, recv_sem = rest[3 * n_parts :]
    dp = lax.axis_index("dp")
    t = lax.axis_index("tensor")
    core = lax.rem(t, 2)
    sign = 1 - 2 * core

    def chip(dz):
        return {"tensor": lax.rem(t + 2 * dz + SLOTS, SLOTS)}

    sibling = {"tensor": t + sign}

    def across(dz):
        return {"tensor": lax.rem(t + sign + 2 * dz + SLOTS, SLOTS)}


    def plane_at(d):
        return lax.rem(dp // 4 + d // 4, 4) * 4 + lax.rem(dp + d, 4)

    def plane(d):
        return {"dp": plane_at(d)}

    offsets = sorted(range(1, DP), key=lambda d: -min(d // 4, 4 - d // 4) - min(d % 4, 4 - d % 4))

    barrier = pltpu.get_barrier_semaphore()
    partners = [sibling] + [chip(dz) for dz in (6, -6, 3, -3, 2, -2, 1, -1)]
    partners += [across(dz) for dz in (-2 * sign, 1, -1)] + [plane(d) for d in offsets]
    for device in partners:
        pl.semaphore_signal(barrier, inc=1, device_id=device, device_id_type=MESH)

    loads = []
    for n, (src, dst) in enumerate(
        ((cot_hbm, cot), (dec_hbm, dec), (q_hbm, q), (k_hbm, k), (v_hbm, v), (pos_hbm, pos), (enc_hbm, enc), (w_hbm, w))
    ):
        c = pltpu.make_async_copy(src, dst, in_sem.at[n])
        c.start()
        loads.append(c)
    cot_in, dec_in, q_in, k_in, v_in, pos_in, enc_in, w_in = loads

    count = [0]
    started = []

    def send(src, dst, device):
        n = count[0]
        count[0] = n + 1
        c = pltpu.make_async_remote_copy(
            src_ref=src, dst_ref=dst, send_sem=send_sem.at[n], recv_sem=recv_sem.at[n],
            device_id=device, device_id_type=MESH,
        )
        c.start()
        started.append(c)
        return c

    cot8[...] = jnp.zeros_like(cot8)
    gst[...] = jnp.zeros_like(gst)
    groups8 = lane_groups(PAD)
    cot_in.wait()
    dec_in.wait()
    cot8[0:OWN, :] = cot[...].astype(F32)
    for j in range(TILES):
        rows = jnp.concatenate([cot8[:, 512 * j + 128 * i : 512 * j + 128 * (i + 1)] for i in range(4)], axis=0)
        full = dot(rows.astype(BF16), dec[4 * j : 4 * j + 4].reshape(128, 128), NT)
        tile = jnp.zeros((PAD, 128), F32)
        for i in range(4):
            tile = tile + jnp.where(groups8 == i, full[PAD * i : PAD * (i + 1)], 0.0)
        gst[OWN * j : OWN * j + PAD, :] = tile
    gbuf[0, 0] = gst[...].astype(BF16)

    row = lax.broadcasted_iota(jnp.int32, (SLOTS * PAD, LEN), 0)
    col = lax.broadcasted_iota(jnp.int32, (SLOTS * PAD, LEN), 1)
    slot = row // PAD
    other = slot // 16
    place = slot % 16
    step = jnp.full_like(row, 8)
    for n in range(15):
        step = jnp.where(place == n, NEAR[n // 5] + FAR[n % 5], step)
    at_chip = (t // 2 + step + 16) % 16
    token = OWN * (2 * at_chip + (core + other) % 2) + row % PAD
    valid = row % PAD < OWN
    perm[...] = jnp.where(valid & (token == col), 1.0, 0.0).astype(BF16)

    q_in.wait()
    k_in.wait()
    v_in.wait()
    pos_in.wait()
    scale = HEAD ** (-0.5)
    qp = dot(perm[...], q[...]).astype(BF16)
    pos8 = jnp.broadcast_to(pos[...].reshape(1, LEN), (PAD, LEN)).astype(F32).astype(BF16)
    pos_col = dot(perm[...], pos8, NT)[:, 0:1].astype(jnp.int32)
    scores = dot(qp, k[...], NT) * scale
    visible = (col <= token) & (col >= token - pos_col)
    scores = jnp.where(visible, scores, F32(-1e30))
    exps = jnp.exp(scores - jnp.max(scores, axis=-1, keepdims=True))
    probs = exps / jnp.sum(exps, axis=-1, keepdims=True)
    attn[...] = probs
    ctx_f = dot(probs.astype(BF16), v[...])
    ctx[...] = ctx_f.astype(BF16)
    ctx_t[...] = ctx_f.T.astype(BF16)

    enc_in.wait()
    code_group = lax.broadcasted_iota(jnp.int32, (128, 128), 0) // 32
    for j in range(TILES):
        group = enc[4 * j : 4 * j + 4].reshape(128, 128)
        for i in range(4):
            spread[j, :, 128 * i : 128 * (i + 1)] = jnp.where(code_group == i, group, jnp.zeros_like(group))

    w_in.wait()
    for j in range(TILES):
        part = dot(w[:, 512 * j : 512 * (j + 1)], spread[j], NT).astype(BF16)
        wenc[:, 128 * j : 128 * (j + 1)] = part
    for j in range(TILES):
        part = dot(ctx[...], wenc[:, 128 * j : 128 * (j + 1)])
        pst[:, OWN * j : OWN * j + PAD, :] = part.reshape(SLOTS, PAD, 128)
    pst[:, MSG - 8 : MSG, :] = jnp.zeros((SLOTS, 8, 128), F32)
    psnd[...] = pst[16:32].astype(BF16)
    pl.semaphore_wait(barrier, len(partners))

    own = gbuf.at[0, 0]
    g_far = {}
    for n in (3, 4, 1, 2):
        back = n + 1 if n % 2 else n - 1
        g_far[n] = send(own, gbuf.at[0, back], chip(FAR[n]))
    g_near = {p: send(own, gbuf.at[0, 5 * p], chip(-NEAR[p])) for p in (1, 2)}
    p_sib = send(psnd, psib, sibling)

    p_sib.wait_recv()
    for n in range(16):
        pst[n] = pst[n] + psib[n].astype(F32)
        if n >= 5:
            pone[n] = pst[n].astype(BF16)
    p_near = [send(pone.at[pl.ds(5 * p, 5)], prec1.at[p], chip(NEAR[p])) for p in (1, 2)]
    p_near.append(send(pone.at[15], prec15, chip(2 * sign)))

    def unpack(other_core):
        ust[...] = gbuf[other_core].astype(F32)
        keep = lax.broadcasted_iota(jnp.int32, (16, PAD, 128), 1) < OWN
        for j in range(TILES):
            block = jnp.where(keep, ust[:, OWN * j : OWN * j + PAD, :], 0.0)
            gpad[128 * other_core : 128 * (other_core + 1), 128 * j : 128 * (j + 1)] = block.reshape(128, 128).astype(BF16)

    g_pack = {}
    for part in (1, 3):
        g_far[part].wait_recv()
        g_far[part + 1].wait_recv()
        for p in (1, 2):
            block = pl.ds(5 * p + part, 2)
            g_pack[p, part] = send(gbuf.at[0, pl.ds(part, 2)], gbuf.at[0, block], chip(-NEAR[p]))
    g_last = [send(gbuf.at[0, 3 + core], gbuf.at[0, 15], chip(-2 * sign))]
    g_last.append(send(gbuf.at[0, 3 + core], gbuf.at[1, 15], across(-2 * sign)))
    for p in (1, 2):
        g_last.append(send(gbuf.at[0, pl.ds(3, 2)], gbuf.at[1, pl.ds(5 * p + 3, 2)], across(-NEAR[p])))
    g_over = [send(gbuf.at[0, pl.ds(0, 5)], gbuf.at[1, pl.ds(0, 5)], sibling)]
    for p in (1, 2):
        g_near[p].wait_recv()
        g_pack[p, 1].wait_recv()
        g_over.append(send(gbuf.at[0, pl.ds(5 * p, 3)], gbuf.at[1, pl.ds(5 * p, 3)], sibling))
    for p in (1, 2):
        g_pack[p, 3].wait_recv()
    g_last[0].wait_recv()
    unpack(0)
    for c in g_over + g_last[1:]:
        c.wait_recv()
    unpack(1)

    m_parts = []
    for (first, wide), part, recv in zip(PARTS, parts, recvs):
        width = 128 * wide
        grad = dot(ctx_t[...], gpad[:, 128 * first : 128 * first + width]).astype(BF16)
        for r in range(DP):
            part[r] = grad[16 * (r // 2) : 16 * (r // 2 + 1), width // 2 * (r % 2) : width // 2 * (r % 2 + 1)]
        m_parts.append([send(part.at[plane_at(d)], recv.at[d], plane(d)) for d in offsets])

    for c in p_near:
        c.wait_recv()
    for n in range(5):
        total = pst[n] + prec1[1, n].astype(F32) + prec1[2, n].astype(F32)
        if n >= 3:
            total = total + jnp.where(core == n - 3, prec15[...].astype(F32), 0.0)
        if n:
            ptwo[n] = total.astype(BF16)
        else:
            code[0:MSG] = total
    p_far = [send(ptwo.at[n], prec2.at[n], chip(FAR[n])) for n in (3, 4, 1, 2)]
    gc = dot(gpad[...], wenc[...], NT).astype(BF16)
    probs = attn[...]
    gv_out[...] = dot(probs.astype(BF16), gc, TN).astype(BF16)
    g_prob = dot(gc, v[...], NT)
    row_dot = jnp.sum(probs * g_prob, axis=-1, keepdims=True)
    g_score = (probs * (g_prob - row_dot) * scale).astype(BF16)
    gq_out[...] = dot(perm[...], dot(g_score, k[...]).astype(BF16), TN).astype(BF16)
    gk_out[...] = dot(g_score, qp, TN).astype(BF16)

    m_sums = []
    for copies, part, recv, full in zip(m_parts, parts, recvs, fulls):
        total = part[dp].astype(F32)
        for d, c in zip(offsets, copies):
            c.wait_recv()
            total = total + recv[d].astype(F32)
        full[dp] = total.astype(BF16)
        m_sums.append([send(full.at[dp], full.at[dp], plane(d)) for d in offsets])

    for c in p_far:
        c.wait_recv()
    total = code[0:MSG]
    for n in (1, 2, 3, 4):
        total = total + prec2[n].astype(F32)
    code[0:MSG] = total
    for j in range(TILES):
        rows = code[OWN * j : OWN * j + PAD, :]
        rows = jnp.concatenate([jnp.where(groups8 == i, rows, 0.0) for i in range(4)], axis=0)
        full = dot(rows.astype(BF16), dec[4 * j : 4 * j + 4].reshape(128, 128))
        for i in range(4):
            att_out[:, 512 * j + 128 * i : 512 * j + 128 * (i + 1)] = full[PAD * i : PAD * i + OWN].astype(BF16)

    for c in started:
        c.wait_send()
    for (first, wide), full, copies in zip(PARTS, fulls, m_sums):
        for c in copies:
            c.wait_recv()
        if first == PARTS[LAST][0]:
            last_out[...] = full[...]
            break
        for j in range(first, first + wide):
            block = enc[4 * j : 4 * j + 4].reshape(128, 128)
            for i, tile in enumerate(expand(full, wide // 2, j - first, block)):
                gw_out[:, 512 * j + 128 * i : 512 * j + 128 * (i + 1)] = tile


def weight_kernel(gw_head, last, enc, att_in, gq_in, gk_in, gv_in, att_out, gq_out, gk_out, gv_out, gw_out, gw, out_sem):
    saves = []
    first, wide = PARTS[LAST]
    head = gw_out.at[:, pl.ds(0, 512 * first)]
    for n, (src, dst) in enumerate(((gw_head, head), (att_in, att_out), (gq_in, gq_out), (gk_in, gk_out), (gv_in, gv_out))):
        c = pltpu.make_async_copy(src, dst, out_sem.at[n])
        c.start()
        saves.append(c)
    for n in range(wide):
        block = enc[4 * (first + n) : 4 * (first + n) + 4].reshape(128, 128)
        for i, tile in enumerate(expand(last, wide // 2, n, block)):
            gw[n, :, 128 * i : 128 * (i + 1)] = tile
        c = pltpu.make_async_copy(gw.at[n], gw_out.at[:, pl.ds(512 * (first + n), 512)], out_sem.at[5 + n])
        c.start()
        saves.append(c)
    for c in saves:
        c.wait()


def local(q, k, v, w, enc, dec, pos, cot):
    any_ = pl.BlockSpec(memory_space=pl.ANY)
    hbm = pl.BlockSpec(memory_space=pltpu.HBM)
    vmem = pl.BlockSpec(memory_space=pltpu.VMEM)

    def shape(*dims):
        return jax.ShapeDtypeStruct(dims, BF16)

    n_copies = 25 + 2 * (DP - 1) * len(PARTS)
    shares = [(DP, 16, 64 * wide) for _, wide in PARTS]
    operands = (q, k, v, w, enc.transpose(0, 2, 1), dec, pos, cot)
    row_shapes = (shape(OWN, WIDTH), shape(LEN, HEAD), shape(LEN, HEAD), shape(LEN, HEAD))
    gw_head, last, att, gq, gk, gv, enc_kept = pl.pallas_call(
        core_kernel,
        out_shape=(shape(HEAD, 512 * PARTS[LAST][0]), shape(*shares[LAST]), *row_shapes, shape(40, 32, 128)),
        in_specs=[hbm] * 8,
        out_specs=[vmem] * 7,
        scratch_shapes=[
            pltpu.VMEM((LEN, HEAD), BF16),
            pltpu.VMEM((LEN, HEAD), BF16),
            pltpu.VMEM((LEN, HEAD), BF16),
            pltpu.VMEM((HEAD, WIDTH), BF16),
            pltpu.VMEM((40, 32, 128), BF16),
            pltpu.VMEM((LEN,), jnp.int32),
            pltpu.VMEM((OWN, WIDTH), BF16),
            pltpu.VMEM((PAD, WIDTH), F32),
            pltpu.VMEM((MSG, 128), F32),
            pltpu.VMEM((2, 16, MSG, 128), BF16),
            pltpu.VMEM((16, MSG, 128), F32),
            pltpu.VMEM((SLOTS * PAD, CODE), BF16),
            pltpu.VMEM((SLOTS * PAD, LEN), BF16),
            pltpu.VMEM((SLOTS * PAD, LEN), F32),
            pltpu.VMEM((SLOTS * PAD, HEAD), BF16),
            pltpu.VMEM((HEAD, SLOTS * PAD), BF16),
            pltpu.VMEM((TILES, 128, 512), BF16),
            pltpu.VMEM((HEAD, CODE), BF16),
            pltpu.VMEM((SLOTS, MSG, 128), F32),
            pltpu.VMEM((16, MSG, 128), BF16),
            pltpu.VMEM((16, MSG, 128), BF16),
            pltpu.VMEM((16, MSG, 128), BF16),
            pltpu.VMEM((3, 5, MSG, 128), BF16),
            pltpu.VMEM((MSG, 128), BF16),
            pltpu.VMEM((5, MSG, 128), BF16),
            pltpu.VMEM((5, MSG, 128), BF16),
            pltpu.VMEM((MSG, 128), F32),
            *[pltpu.VMEM(share, BF16) for share in 3 * shares],
            pltpu.SemaphoreType.DMA((8,)),
            pltpu.SemaphoreType.DMA((n_copies,)),
            pltpu.SemaphoreType.DMA((n_copies,)),
        ],
        compiler_params=pltpu.CompilerParams(
            collective_id=0, has_side_effects=True, vmem_limit_bytes=48 * 2**20
        ),
        name="attention_and_sums",
    )(*[pltpu.with_memory_space_constraint(a, pltpu.HBM) for a in operands])
    return pl.pallas_call(
        weight_kernel,
        out_shape=(*row_shapes, shape(HEAD, WIDTH)),
        in_specs=[vmem] * 7,
        out_specs=[any_] * 5,
        scratch_shapes=[
            pltpu.VMEM((PARTS[LAST][1], HEAD, 512), BF16),
            pltpu.SemaphoreType.DMA((5 + PARTS[LAST][1],)),
        ],
        compiler_params=pltpu.CompilerParams(vmem_limit_bytes=16 * 2**20),
        name="weight_gradient",
    )(gw_head, last, enc_kept, att, gq, gk, gv)


def solution(mesh):
    return jax.shard_map(
        local,
        mesh=mesh,
        in_specs=(
            P("dp", "tensor"), P("dp", "tensor"), P("dp", "tensor"), P("tensor", None),
            P(), P(), P("dp"), P(("dp", "tensor"), None),
        ),
        out_specs=(
            P(("dp", "tensor"), None), P("dp", "tensor"), P("dp", "tensor"), P("dp", "tensor"), P("tensor", None),
        ),
        check_vma=False,
    )
```

```python
import functools

import jax
import jax.numpy as jnp
from jax import lax
from jax.experimental import pallas as pl
from jax.experimental.pallas import tpu as pltpu
from jax.sharding import PartitionSpec as P

MESH = pl.DeviceIdType.MESH
F32 = jnp.float32
BF16 = jnp.bfloat16

LEN = 160
HEAD = 128
WIDTH = 5120
CODE = 1280
TILES = CODE // 128
OWN = 5
PAD = 8
SLOTS = 32
MSG = 64
DP = 16
NT = (((1,), (1,)), ((), ()))
TN = (((0,), (0,)), ((), ()))
NEAR = (0, 1, -1)
FAR = (0, 3, -3, 6, -6)
PARTS = ((0, 4), (4, 6))
LAST = len(PARTS) - 1


def dot(a, b, dims=(((1,), (0,)), ((), ()))):
    return lax.dot_general(a, b, dims, preferred_element_type=F32)


def lane_groups(rows):
    return lax.broadcasted_iota(jnp.int32, (rows, 128), 1) // 32


def expand(sums, wide, at, block):
    half, place = at // wide, at % wide
    rows = jnp.concatenate([sums[2 * r + half, :, 128 * place : 128 * (place + 1)] for r in range(8)], axis=0)
    groups = lane_groups(HEAD)
    return [dot(jnp.where(groups == i, rows, jnp.zeros_like(rows)), block).astype(BF16) for i in range(4)]


def core_kernel(
    q_hbm, k_hbm, v_hbm, w_hbm, enc_hbm, dec_hbm, pos_hbm, cot_hbm,
    gw_out, last_out, att_out, gq_out, gk_out, gv_out, enc,
    q, k, v, w, dec, pos, cot, cot8, gst, gbuf, ust, gpad, perm, attn, ctx, ctx_t, spread, wenc,
    pst, psnd, psib, pone, prec1, prec15, ptwo, prec2, code, *rest,
):
    n_parts = len(PARTS)
    parts, recvs, fulls = rest[:n_parts], rest[n_parts : 2 * n_parts], rest[2 * n_parts : 3 * n_parts]
    in_sem, send_sem, recv_sem = rest[3 * n_parts :]
    dp = lax.axis_index("dp")
    t = lax.axis_index("tensor")
    core = lax.rem(t, 2)
    sign = 1 - 2 * core

    def chip(dz):
        return {"tensor": lax.rem(t + 2 * dz + SLOTS, SLOTS)}

    sibling = {"tensor": t + sign}

    def across(dz):
        return {"tensor": lax.rem(t + sign + 2 * dz + SLOTS, SLOTS)}


    def plane_at(d):
        return lax.rem(dp // 4 + d // 4, 4) * 4 + lax.rem(dp + d, 4)

    def plane(d):
        return {"dp": plane_at(d)}

    offsets = sorted(range(1, DP), key=lambda d: -min(d // 4, 4 - d // 4) - min(d % 4, 4 - d % 4))

    barrier = pltpu.get_barrier_semaphore()
    partners = [sibling] + [chip(dz) for dz in (6, -6, 3, -3, 2, -2, 1, -1)]
    partners += [across(dz) for dz in (-2 * sign, 1, -1)] + [plane(d) for d in offsets]
    for device in partners:
        pl.semaphore_signal(barrier, inc=1, device_id=device, device_id_type=MESH)

    loads = []
    for n, (src, dst) in enumerate(
        ((cot_hbm, cot), (dec_hbm, dec), (q_hbm, q), (k_hbm, k), (v_hbm, v), (pos_hbm, pos), (enc_hbm, enc), (w_hbm, w))
    ):
        c = pltpu.make_async_copy(src, dst, in_sem.at[n])
        c.start()
        loads.append(c)
    cot_in, dec_in, q_in, k_in, v_in, pos_in, enc_in, w_in = loads

    count = [0]
    started = []

    def send(src, dst, device):
        n = count[0]
        count[0] = n + 1
        c = pltpu.make_async_remote_copy(
            src_ref=src, dst_ref=dst, send_sem=send_sem.at[n], recv_sem=recv_sem.at[n],
            device_id=device, device_id_type=MESH,
        )
        c.start()
        started.append(c)
        return c

    cot8[...] = jnp.zeros_like(cot8)
    gst[...] = jnp.zeros_like(gst)
    groups8 = lane_groups(PAD)
    cot_in.wait()
    dec_in.wait()
    cot8[0:OWN, :] = cot[...].astype(F32)
    for j in range(TILES):
        rows = jnp.concatenate([cot8[:, 512 * j + 128 * i : 512 * j + 128 * (i + 1)] for i in range(4)], axis=0)
        full = dot(rows.astype(BF16), dec[4 * j : 4 * j + 4].reshape(128, 128), NT)
        tile = jnp.zeros((PAD, 128), F32)
        for i in range(4):
            tile = tile + jnp.where(groups8 == i, full[PAD * i : PAD * (i + 1)], 0.0)
        gst[OWN * j : OWN * j + PAD, :] = tile
    gbuf[0, 0] = gst[...].astype(BF16)

    row = lax.broadcasted_iota(jnp.int32, (SLOTS * PAD, LEN), 0)
    col = lax.broadcasted_iota(jnp.int32, (SLOTS * PAD, LEN), 1)
    slot = row // PAD
    other = slot // 16
    place = slot % 16
    step = jnp.full_like(row, 8)
    for n in range(15):
        step = jnp.where(place == n, NEAR[n // 5] + FAR[n % 5], step)
    at_chip = (t // 2 + step + 16) % 16
    token = OWN * (2 * at_chip + (core + other) % 2) + row % PAD
    valid = row % PAD < OWN
    perm[...] = jnp.where(valid & (token == col), 1.0, 0.0).astype(BF16)

    q_in.wait()
    k_in.wait()
    v_in.wait()
    pos_in.wait()
    scale = HEAD ** (-0.5)
    qp = dot(perm[...], q[...]).astype(BF16)
    pos8 = jnp.broadcast_to(pos[...].reshape(1, LEN), (PAD, LEN)).astype(F32).astype(BF16)
    pos_col = dot(perm[...], pos8, NT)[:, 0:1].astype(jnp.int32)
    scores = dot(qp, k[...], NT) * scale
    visible = (col <= token) & (col >= token - pos_col)
    scores = jnp.where(visible, scores, F32(-1e30))
    exps = jnp.exp(scores - jnp.max(scores, axis=-1, keepdims=True))
    probs = exps / jnp.sum(exps, axis=-1, keepdims=True)
    attn[...] = probs
    ctx_f = dot(probs.astype(BF16), v[...])
    ctx[...] = ctx_f.astype(BF16)
    ctx_t[...] = ctx_f.T.astype(BF16)

    enc_in.wait()
    code_group = lax.broadcasted_iota(jnp.int32, (128, 128), 0) // 32
    for j in range(TILES):
        group = enc[4 * j : 4 * j + 4].reshape(128, 128)
        for i in range(4):
            spread[j, :, 128 * i : 128 * (i + 1)] = jnp.where(code_group == i, group, jnp.zeros_like(group))

    w_in.wait()
    for j in range(TILES):
        part = dot(w[:, 512 * j : 512 * (j + 1)], spread[j], NT).astype(BF16)
        wenc[:, 128 * j : 128 * (j + 1)] = part
    for j in range(TILES):
        part = dot(ctx[...], wenc[:, 128 * j : 128 * (j + 1)])
        pst[:, OWN * j : OWN * j + PAD, :] = part.reshape(SLOTS, PAD, 128)
    pst[:, MSG - 8 : MSG, :] = jnp.zeros((SLOTS, 8, 128), F32)
    psnd[...] = pst[16:32].astype(BF16)
    pl.semaphore_wait(barrier, len(partners))

    own = gbuf.at[0, 0]
    g_far = {}
    for n in (3, 4, 1, 2):
        back = n + 1 if n % 2 else n - 1
        g_far[n] = send(own, gbuf.at[0, back], chip(FAR[n]))
    g_near = {p: send(own, gbuf.at[0, 5 * p], chip(-NEAR[p])) for p in (1, 2)}
    p_sib = send(psnd, psib, sibling)

    p_sib.wait_recv()
    for n in range(16):
        pst[n] = pst[n] + psib[n].astype(F32)
        if n >= 5:
            pone[n] = pst[n].astype(BF16)
    p_near = [send(pone.at[pl.ds(5 * p, 5)], prec1.at[p], chip(NEAR[p])) for p in (1, 2)]
    p_near.append(send(pone.at[15], prec15, chip(2 * sign)))

    def unpack(other_core):
        ust[...] = gbuf[other_core].astype(F32)
        keep = lax.broadcasted_iota(jnp.int32, (16, PAD, 128), 1) < OWN
        for j in range(TILES):
            block = jnp.where(keep, ust[:, OWN * j : OWN * j + PAD, :], 0.0)
            gpad[128 * other_core : 128 * (other_core + 1), 128 * j : 128 * (j + 1)] = block.reshape(128, 128).astype(BF16)

    g_pack = {}
    for part in (1, 3):
        g_far[part].wait_recv()
        g_far[part + 1].wait_recv()
        for p in (1, 2):
            block = pl.ds(5 * p + part, 2)
            g_pack[p, part] = send(gbuf.at[0, pl.ds(part, 2)], gbuf.at[0, block], chip(-NEAR[p]))
    g_last = [send(gbuf.at[0, 3 + core], gbuf.at[0, 15], chip(-2 * sign))]
    g_last.append(send(gbuf.at[0, 3 + core], gbuf.at[1, 15], across(-2 * sign)))
    for p in (1, 2):
        g_last.append(send(gbuf.at[0, pl.ds(3, 2)], gbuf.at[1, pl.ds(5 * p + 3, 2)], across(-NEAR[p])))
    g_over = [send(gbuf.at[0, pl.ds(0, 5)], gbuf.at[1, pl.ds(0, 5)], sibling)]
    for p in (1, 2):
        g_near[p].wait_recv()
        g_pack[p, 1].wait_recv()
        g_over.append(send(gbuf.at[0, pl.ds(5 * p, 3)], gbuf.at[1, pl.ds(5 * p, 3)], sibling))
    for p in (1, 2):
        g_pack[p, 3].wait_recv()
    g_last[0].wait_recv()
    unpack(0)
    for c in g_over + g_last[1:]:
        c.wait_recv()
    unpack(1)

    m_parts = []
    for (first, wide), part, recv in zip(PARTS, parts, recvs):
        width = 128 * wide
        grad = dot(ctx_t[...], gpad[:, 128 * first : 128 * first + width]).astype(BF16)
        for r in range(DP):
            part[r] = grad[16 * (r // 2) : 16 * (r // 2 + 1), width // 2 * (r % 2) : width // 2 * (r % 2 + 1)]
        m_parts.append([send(part.at[plane_at(d)], recv.at[d], plane(d)) for d in offsets])

    for c in p_near:
        c.wait_recv()
    for n in range(5):
        total = pst[n] + prec1[1, n].astype(F32) + prec1[2, n].astype(F32)
        if n >= 3:
            total = total + jnp.where(core == n - 3, prec15[...].astype(F32), 0.0)
        if n:
            ptwo[n] = total.astype(BF16)
        else:
            code[0:MSG] = total
    p_far = [send(ptwo.at[n], prec2.at[n], chip(FAR[n])) for n in (3, 4, 1, 2)]
    gc = dot(gpad[...], wenc[...], NT).astype(BF16)
    probs = attn[...]
    gv_out[...] = dot(probs.astype(BF16), gc, TN).astype(BF16)
    g_prob = dot(gc, v[...], NT)
    row_dot = jnp.sum(probs * g_prob, axis=-1, keepdims=True)
    g_score = (probs * (g_prob - row_dot) * scale).astype(BF16)
    gq_out[...] = dot(perm[...], dot(g_score, k[...]).astype(BF16), TN).astype(BF16)
    gk_out[...] = dot(g_score, qp, TN).astype(BF16)

    m_sums = []
    for copies, part, recv, full in zip(m_parts, parts, recvs, fulls):
        total = part[dp].astype(F32)
        for d, c in zip(offsets, copies):
            c.wait_recv()
            total = total + recv[d].astype(F32)
        full[dp] = total.astype(BF16)
        m_sums.append([send(full.at[dp], full.at[dp], plane(d)) for d in offsets])

    for c in started:
        c.wait_send()
    for (first, wide), full, copies in zip(PARTS[:LAST], fulls, m_sums):
        for c in copies:
            c.wait_recv()
        for j in range(first, first + wide):
            block = enc[4 * j : 4 * j + 4].reshape(128, 128)
            for i, tile in enumerate(expand(full, wide // 2, j - first, block)):
                gw_out[:, 512 * j + 128 * i : 512 * j + 128 * (i + 1)] = tile
    for c in p_far:
        c.wait_recv()
    total = code[0:MSG]
    for n in (1, 2, 3, 4):
        total = total + prec2[n].astype(F32)
    code[0:MSG] = total
    for j in range(TILES):
        rows = code[OWN * j : OWN * j + PAD, :]
        rows = jnp.concatenate([jnp.where(groups8 == i, rows, 0.0) for i in range(4)], axis=0)
        full = dot(rows.astype(BF16), dec[4 * j : 4 * j + 4].reshape(128, 128))
        for i in range(4):
            att_out[:, 512 * j + 128 * i : 512 * j + 128 * (i + 1)] = full[PAD * i : PAD * i + OWN].astype(BF16)
    for c in m_sums[LAST]:
        c.wait_recv()
    last_out[...] = fulls[LAST][...]


def weight_kernel(gw_head, last, enc, att_in, gq_in, gk_in, gv_in, att_out, gq_out, gk_out, gv_out, gw_out, gw, out_sem):
    saves = []
    first, wide = PARTS[LAST]
    head = gw_out.at[:, pl.ds(0, 512 * first)]
    for n, (src, dst) in enumerate(((gw_head, head), (att_in, att_out), (gq_in, gq_out), (gk_in, gk_out), (gv_in, gv_out))):
        c = pltpu.make_async_copy(src, dst, out_sem.at[n])
        c.start()
        saves.append(c)
    for n in range(wide):
        block = enc[4 * (first + n) : 4 * (first + n) + 4].reshape(128, 128)
        for i, tile in enumerate(expand(last, wide // 2, n, block)):
            gw[n, :, 128 * i : 128 * (i + 1)] = tile
        c = pltpu.make_async_copy(gw.at[n], gw_out.at[:, pl.ds(512 * (first + n), 512)], out_sem.at[5 + n])
        c.start()
        saves.append(c)
    for c in saves:
        c.wait()


def local(q, k, v, w, enc, dec, pos, cot):
    any_ = pl.BlockSpec(memory_space=pl.ANY)
    hbm = pl.BlockSpec(memory_space=pltpu.HBM)
    vmem = pl.BlockSpec(memory_space=pltpu.VMEM)

    def shape(*dims):
        return jax.ShapeDtypeStruct(dims, BF16)

    n_copies = 25 + 2 * (DP - 1) * len(PARTS)
    shares = [(DP, 16, 64 * wide) for _, wide in PARTS]
    operands = (q, k, v, w, enc.transpose(0, 2, 1), dec, pos, cot)
    row_shapes = (shape(OWN, WIDTH), shape(LEN, HEAD), shape(LEN, HEAD), shape(LEN, HEAD))
    gw_head, last, att, gq, gk, gv, enc_kept = pl.pallas_call(
        core_kernel,
        out_shape=(shape(HEAD, 512 * PARTS[LAST][0]), shape(*shares[LAST]), *row_shapes, shape(40, 32, 128)),
        in_specs=[hbm] * 8,
        out_specs=[vmem] * 7,
        scratch_shapes=[
            pltpu.VMEM((LEN, HEAD), BF16),
            pltpu.VMEM((LEN, HEAD), BF16),
            pltpu.VMEM((LEN, HEAD), BF16),
            pltpu.VMEM((HEAD, WIDTH), BF16),
            pltpu.VMEM((40, 32, 128), BF16),
            pltpu.VMEM((LEN,), jnp.int32),
            pltpu.VMEM((OWN, WIDTH), BF16),
            pltpu.VMEM((PAD, WIDTH), F32),
            pltpu.VMEM((MSG, 128), F32),
            pltpu.VMEM((2, 16, MSG, 128), BF16),
            pltpu.VMEM((16, MSG, 128), F32),
            pltpu.VMEM((SLOTS * PAD, CODE), BF16),
            pltpu.VMEM((SLOTS * PAD, LEN), BF16),
            pltpu.VMEM((SLOTS * PAD, LEN), F32),
            pltpu.VMEM((SLOTS * PAD, HEAD), BF16),
            pltpu.VMEM((HEAD, SLOTS * PAD), BF16),
            pltpu.VMEM((TILES, 128, 512), BF16),
            pltpu.VMEM((HEAD, CODE), BF16),
            pltpu.VMEM((SLOTS, MSG, 128), F32),
            pltpu.VMEM((16, MSG, 128), BF16),
            pltpu.VMEM((16, MSG, 128), BF16),
            pltpu.VMEM((16, MSG, 128), BF16),
            pltpu.VMEM((3, 5, MSG, 128), BF16),
            pltpu.VMEM((MSG, 128), BF16),
            pltpu.VMEM((5, MSG, 128), BF16),
            pltpu.VMEM((5, MSG, 128), BF16),
            pltpu.VMEM((MSG, 128), F32),
            *[pltpu.VMEM(share, BF16) for share in 3 * shares],
            pltpu.SemaphoreType.DMA((8,)),
            pltpu.SemaphoreType.DMA((n_copies,)),
            pltpu.SemaphoreType.DMA((n_copies,)),
        ],
        compiler_params=pltpu.CompilerParams(
            collective_id=0, has_side_effects=True, vmem_limit_bytes=48 * 2**20
        ),
        name="attention_and_sums",
    )(*[pltpu.with_memory_space_constraint(a, pltpu.HBM) for a in operands])
    return pl.pallas_call(
        weight_kernel,
        out_shape=(*row_shapes, shape(HEAD, WIDTH)),
        in_specs=[vmem] * 7,
        out_specs=[any_] * 5,
        scratch_shapes=[
            pltpu.VMEM((PARTS[LAST][1], HEAD, 512), BF16),
            pltpu.SemaphoreType.DMA((5 + PARTS[LAST][1],)),
        ],
        compiler_params=pltpu.CompilerParams(vmem_limit_bytes=16 * 2**20),
        name="weight_gradient",
    )(gw_head, last, enc_kept, att, gq, gk, gv)


def solution(mesh):
    return jax.shard_map(
        local,
        mesh=mesh,
        in_specs=(
            P("dp", "tensor"), P("dp", "tensor"), P("dp", "tensor"), P("tensor", None),
            P(), P(), P("dp"), P(("dp", "tensor"), None),
        ),
        out_specs=(
            P(("dp", "tensor"), None), P("dp", "tensor"), P("dp", "tensor"), P("dp", "tensor"), P("tensor", None),
        ),
        check_vma=False,
    )
```
